32 devices in a mesh: fsdp: 4 (over y, x), seq: 8 (over z, core).
Axes of the slice: x: 2, y: 2, z: 4, core: 2. Of those that a mesh axis runs over, the one named last changes fastest.
Arguments:
- hidden: bfloat16 [4, 1024, 5120], P('fsdp', 'seq'), may hold values from -6 to 6
- queries: bfloat16 [4, 1024, 4096], P('fsdp', 'seq'), may hold values from -400 to 400
- key_value_weight: bfloat16 [5120, 2048], P('fsdp'), may hold values from -0.078125 to 0.078125
- doc_lengths: int32 [4, 8], P('fsdp'), may hold values from 1 to 512, 1024 in all within a row
- resp_lengths: int32 [4, 8], P('fsdp'), may hold values from 1 to 128
Outputs:
- attended: bfloat16 [4, 1024, 4096], P('fsdp', 'seq')
- pooled: float32 [4, 8, 4096], P('fsdp', None, 'seq')
The draws below stay inside these ranges and needn't reach their ends.
Inputs may be any that keep to these rules, and one draw needn't show every extreme that they name: `doc_lengths`: each row holds the lengths of the documents of one packed sequence in order; they sum to 1024 and the longest is exactly 512.
All inputs are finite; a program needn't handle non-finite values.
Results may differ from the reference program's by a relative error of at most 0.011.
Values may be sent and summed in bfloat16 or wider, within the bound.
A program may use at most 128 MiB of HBM per device.

```python
import math
import jax
import jax.numpy as jnp
import numpy as np
from jax import lax

MODEL_WIDTH = 5120
HEAD_SIZE = 128
KEY_VALUE_HEADS = 8
QUERY_HEADS = 32
TOK_DEV = 128
BATCH = 4
PACKED_LENGTH = 1024
DOCS = 8
DOC_MAX = 512


def draw_queries(key, part):
    base = jnp.clip(jax.random.normal(key, (BATCH, PACKED_LENGTH, QUERY_HEADS, HEAD_SIZE), jnp.float32), -6.0, 6.0)
    return base.reshape(BATCH, PACKED_LENGTH, QUERY_HEADS * HEAD_SIZE).astype(jnp.bfloat16)


def plant(entries, stream_key, low, high):
    longest = entries.shape.index(max(entries.shape))
    spots = []
    for shift in (0, 1):
        where = [jax.random.randint(jax.random.fold_in(stream_key, axis), (), 0, length) for axis, length in enumerate(entries.shape)]
        where[longest] = (where[longest] + shift) % entries.shape[longest]
        spots.append(tuple(where))
    return entries.at[spots[0]].set(low).at[spots[1]].set(high)


def shard_levels(own_key, dims, split, least, high):
    factor_of = 1.0
    for axis_at, shards_of in split:
        draws = jax.random.uniform(jax.random.fold_in(jax.random.fold_in(own_key, 6), axis_at), (shards_of,), jnp.float32, least / len(split), high / len(split))
        factor_of = factor_of * jnp.repeat(jnp.exp(draws), dims[axis_at] // shards_of).reshape((-1,) + (1,) * (len(dims) - 1 - axis_at))
    return factor_of


def profile(number_of, total, bound, lean):
    loads = [(1 << 20) // math.isqrt(grade ** lean) + 1 for grade in range(2, number_of + 1)]
    rest, counts = total - bound - (number_of - 1), [1] * (number_of - 1)
    while rest > 0:
        free = [i for i in range(number_of - 1) if counts[i] < bound]
        whole, left = sum([loads[i] for i in free]), rest
        for i in free:
            addition = min(bound - counts[i], max(1, left * loads[i] // whole), rest)
            counts[i] = counts[i] + addition
            rest = rest - addition
    return np.array([bound] + counts)


def uneven(rng, amount, total, most, slope):
    if amount == 2:
        one = jax.random.randint(rng, (), max(1, total - most), min(most, total - 1) + 1)
        return jnp.stack([one, total - one])
    sizes = jnp.asarray(profile(amount, total, most, slope), jnp.int32)
    pairs = (amount - 1) // 2
    donor, taker = sizes[1:1 + 2 * pairs:2], sizes[2:2 + 2 * pairs:2]
    slack = jnp.minimum(donor - 1, most - taker)
    moved = jax.random.randint(jax.random.fold_in(rng, 1), (pairs,), 0, 1 << 20) % (slack + 1)
    sizes = sizes.at[1:1 + 2 * pairs:2].set(donor - moved).at[2:2 + 2 * pairs:2].set(taker + moved)
    return sizes[jax.random.permutation(jax.random.fold_in(rng, 2), amount)]


def noise(stream_key, shape, spread, limit, shards=(), held_as=jnp.bfloat16):
    level = shard_levels(stream_key, shape, shards, -0.22, 0.18) if shards else 1.0
    result = jax.random.normal(stream_key, shape, jnp.float32) * spread * level
    return jnp.minimum(jnp.maximum(result, -limit), limit).astype(held_as)


def setup_inputs(seed: int = 0) -> dict:
    key_list = jax.random.split(jax.random.key(seed), 6)
    return {
        "hidden": noise(key_list[0], (BATCH, PACKED_LENGTH, MODEL_WIDTH), 1.0, 6.0, ((0, 4), (1, 8))),
        "queries": draw_queries(jax.random.fold_in(key_list[5], 71), 0),
        "key_value_weight": noise(key_list[2], (MODEL_WIDTH, 2 * KEY_VALUE_HEADS * HEAD_SIZE), MODEL_WIDTH ** -0.5, 0.078125, ((0, 4),)),
        "doc_lengths": jax.vmap(lambda own: uneven(own, DOCS, PACKED_LENGTH, DOC_MAX, 2))(jax.random.split(key_list[3], BATCH)).reshape((BATCH, DOCS)).astype(jnp.int32),
        "resp_lengths": plant(jax.random.randint(key_list[4], (BATCH, DOCS), 1, TOK_DEV + 1), jax.random.fold_in(key_list[4], 1), 1, TOK_DEV).astype(jnp.int32),
    }


ROPE_BASE = 1000000.0


def token_tables(lengths, wanted, first, count):
    ends = jnp.cumsum(lengths).astype(jnp.int32)
    starts = ends - lengths
    answer = jnp.minimum(wanted, lengths)
    index = first + jnp.arange(count, dtype=jnp.int32)
    inside = (index[:, None] >= starts[None, :]) & (index[:, None] < ends[None, :])
    token_position = jnp.sum(jnp.where(inside, index[:, None] - starts[None, :], 0), axis=1).astype(jnp.int32)
    doc_id = jnp.sum(jnp.where(index[:, None] >= ends[None, :], 1, 0), axis=1).astype(jnp.int32)
    member = jnp.where(inside & (index[:, None] >= (ends - answer)[None, :]), 1, 0).astype(jnp.int32)
    return token_position, doc_id, member, answer


def rotate_pairs(heads, token_position):
    half = heads.shape[-1] // 2
    freq = ROPE_BASE ** (-(jnp.arange(half, dtype=jnp.float32) * 2.0 / heads.shape[-1]))
    angle = token_position.astype(jnp.float32)[:, None] * freq[None, :]
    cosine = jnp.cos(angle)[:, None, :]
    sine = jnp.sin(angle)[:, None, :]
    first = heads[..., :half]
    second = heads[..., half:]
    return jnp.concatenate([first * cosine - second * sine, second * cosine + first * sine], axis=-1)


def one_sequence(hidden_row, single_query, key_value_weight, lengths, wanted):
    token_position, doc_id, member, answer = token_tables(lengths, wanted, jnp.int32(0), PACKED_LENGTH)
    projected_rows = jnp.dot(hidden_row, key_value_weight, preferred_element_type=jnp.float32)
    key_rows = rotate_pairs(projected_rows[:, :KEY_VALUE_HEADS * HEAD_SIZE].reshape(PACKED_LENGTH, KEY_VALUE_HEADS, HEAD_SIZE), token_position).astype(jnp.bfloat16)
    value_rows = projected_rows[:, KEY_VALUE_HEADS * HEAD_SIZE:].reshape(PACKED_LENGTH, KEY_VALUE_HEADS, HEAD_SIZE).astype(jnp.bfloat16)
    query_group = QUERY_HEADS // KEY_VALUE_HEADS
    query_matrix = single_query.reshape(PACKED_LENGTH, KEY_VALUE_HEADS, query_group, HEAD_SIZE)
    block = min(512, PACKED_LENGTH)
    window = min(PACKED_LENGTH, block + DOC_MAX)

    def attend(index):
        qstart = index * block
        kstart = jnp.maximum(qstart + block - window, 0).astype(jnp.int32)
        qblock = lax.dynamic_slice_in_dim(query_matrix, qstart, block, 0).astype(jnp.float32)
        kblock = lax.dynamic_slice_in_dim(key_rows, kstart, window, 0).astype(jnp.float32)
        vblock = lax.dynamic_slice_in_dim(value_rows, kstart, window, 0).astype(jnp.float32)
        qdoc = lax.dynamic_slice_in_dim(doc_id, qstart, block, 0)
        kdoc = lax.dynamic_slice_in_dim(doc_id, kstart, window, 0)
        qplace = qstart + jnp.arange(block, dtype=jnp.int32)
        kplace = kstart + jnp.arange(window, dtype=jnp.int32)
        allowed = (qdoc[:, None] == kdoc[None, :]) & (kplace[None, :] <= qplace[:, None])
        scores = jnp.einsum("qkgd,skd->kgqs", qblock, kblock) * (HEAD_SIZE ** -0.5)
        scores = jnp.where(allowed, scores, -1e30)
        peak = jnp.max(scores, axis=-1, keepdims=True)
        weight = jnp.where(allowed, jnp.exp(scores - peak), 0.0)
        probs = (weight / jnp.sum(weight, axis=-1, keepdims=True)).astype(jnp.bfloat16)
        output = jnp.einsum("kgqs,skd->qkgd", probs.astype(jnp.float32), vblock)
        return output.astype(jnp.bfloat16).reshape(block, QUERY_HEADS * HEAD_SIZE)

    attended = lax.map(attend, jnp.arange(PACKED_LENGTH // block, dtype=jnp.int32)).reshape(PACKED_LENGTH, QUERY_HEADS * HEAD_SIZE)
    sums = jnp.einsum("tr,tc->rc", member.astype(jnp.float32), attended.astype(jnp.float32))
    pooled = sums / answer.astype(jnp.float32)[:, None]
    return attended, pooled


def reference(hidden, queries, key_value_weight, doc_lengths, resp_lengths):
    def per_row(items):
        return one_sequence(items[0], items[1], key_value_weight, items[2], items[3])

    attended, pooled = lax.map(per_row, (hidden, queries, doc_lengths, resp_lengths))
    return attended, pooled
```

```python
import functools
import math

import jax
import jax.numpy as jnp
import numpy as np
from jax import lax
from jax.experimental import pallas as pl
from jax.experimental.pallas import tpu as pltpu
from jax.sharding import PartitionSpec as P

HEAD_SIZE = 128
KEY_VALUE_HEADS = 8
ROPE_BASE = 1000000.0
MASKED = -1e30
MESH = pl.DeviceIdType.MESH


def kernel(
    n,
    ranks,
    hops,
    hidden,
    queries,
    weight,
    lengths,
    wanted,
    freq,
    attended,
    pooled,
    x,
    w,
    q,
    product,
    own,
    outbox,
    inbox,
    kv,
    o,
    bias,
    cosine,
    sine,
    member,
    answers,
    part,
    parts,
    x_sem,
    w_sem,
    q_sem,
    o_sem,
    hid_send,
    hid_recv,
    sum_send,
    sum_recv,
    up_send,
    up_recv,
    pair_send,
    pair_recv,
    pool_send,
    pool_recv,
):
    f = lax.axis_index("fsdp")
    s = lax.axis_index("seq")
    odd = lax.rem(s, 2)
    partner = s + 1 - 2 * odd
    above = lax.rem(s + 2, ranks)
    tokens = x.shape[1]
    depth = x.shape[2]
    half = weight.shape[1] // 2
    q_width = q.shape[2]
    docs = lengths.shape[1]
    blocks = kv.shape[0]
    pool_width = part.shape[2]
    per_head = q_width // pool_width

    def columns(start, size):
        return pl.ds(pl.multiple_of(start, HEAD_SIZE), size)

    def features(j):
        if len(hidden.shape) == 3 and hidden.shape[0] == n and n > 1:
            return hidden.at[j]
        return hidden.at[0, :, columns(j * depth, depth)]

    def w_copy(h, side):
        return pltpu.make_async_copy(
            weight.at[:, columns(side * half + h * HEAD_SIZE, HEAD_SIZE)],
            w.at[h, :, pl.ds(side * HEAD_SIZE, HEAD_SIZE)],
            w_sem.at[h, side],
        )

    def q_copy(h):
        return pltpu.make_async_copy(
            queries.at[0, :, columns(h * q_width, q_width)], q.at[h], q_sem.at[h]
        )

    def o_copy(h):
        return pltpu.make_async_copy(
            o.at[h], attended.at[0, :, columns(h * q_width, q_width)], o_sem.at[h]
        )

    def hid_copy(k):
        j = lax.rem(f + k, n)
        return pltpu.make_async_remote_copy(
            src_ref=features(j),
            dst_ref=x.at[f],
            send_sem=hid_send.at[k],
            recv_sem=hid_recv.at[f],
            device_id=(j, s),
            device_id_type=MESH,
        )

    def hid_arrival(k):
        i = lax.rem(f + k, n)
        return pltpu.make_async_remote_copy(
            src_ref=x.at[i],
            dst_ref=x.at[i],
            send_sem=hid_send.at[k],
            recv_sem=hid_recv.at[i],
            device_id=(i, s),
            device_id_type=MESH,
        )

    def sum_copy(h, k):
        j = lax.rem(f + k, n)
        return pltpu.make_async_remote_copy(
            src_ref=outbox.at[h, j],
            dst_ref=inbox.at[h, f],
            send_sem=sum_send.at[h, k],
            recv_sem=sum_recv.at[h, f],
            device_id=(j, s),
            device_id_type=MESH,
        )

    def sum_arrival(h, k):
        i = lax.rem(f + k, n)
        return pltpu.make_async_remote_copy(
            src_ref=outbox.at[h, i],
            dst_ref=inbox.at[h, i],
            send_sem=sum_send.at[h, k],
            recv_sem=sum_recv.at[h, i],
            device_id=(i, s),
            device_id_type=MESH,
        )

    def up_copy(h, i):
        return pltpu.make_async_remote_copy(
            src_ref=kv.at[2 * i, h],
            dst_ref=kv.at[2 * i + 2, h],
            send_sem=up_send.at[h, i],
            recv_sem=up_recv.at[h, i],
            device_id=(f, above),
            device_id_type=MESH,
        )

    def pair_copy(h, source, m):
        return pltpu.make_async_remote_copy(
            src_ref=kv.at[source, h],
            dst_ref=kv.at[2 * m + 1, h],
            send_sem=pair_send.at[h, m],
            recv_sem=pair_recv.at[h, m],
            device_id=(f, partner),
            device_id_type=MESH,
        )

    def pool_copy(j):
        return pltpu.make_async_remote_copy(
            src_ref=part.at[j],
            dst_ref=parts.at[s],
            send_sem=pool_send.at[j],
            recv_sem=pool_recv.at[s],
            device_id=(f, j),
            device_id_type=MESH,
        )

    def pool_arrival(i):
        return pltpu.make_async_remote_copy(
            src_ref=part.at[i],
            dst_ref=parts.at[i],
            send_sem=pool_send.at[i],
            recv_sem=pool_recv.at[i],
            device_id=(f, i),
            device_id_type=MESH,
        )

    def sends_up(i):
        return (s + 2 < ranks) & (s >= 2 * i)

    def shares_even(m):
        return (odd == 0) & (s >= 2 * m)

    def shares_odd(m):
        return (odd == 1) & (s >= 2 * m + 2)

    own_x = pltpu.make_async_copy(features(f), x.at[f], x_sem)
    own_x.start()

    barrier = pltpu.get_barrier_semaphore()
    for k in range(1, n):
        pl.semaphore_signal(
            barrier, inc=1, device_id=(lax.rem(f + k, n), s), device_id_type=MESH
        )
    for k in range(1, ranks):
        pl.semaphore_signal(
            barrier, inc=1, device_id=(f, lax.rem(s + k, ranks)), device_id_type=MESH
        )
    pl.semaphore_wait(barrier, n + ranks - 2)
    for k in range(1, n):
        hid_copy(k).start()

    @pl.loop(0, KEY_VALUE_HEADS)
    def _(h):
        w_copy(h, 0).start()
        w_copy(h, 1).start()

    @pl.loop(0, KEY_VALUE_HEADS)
    def _(h):
        q_copy(h).start()

    ends = []
    total = jnp.int32(0)
    for r in range(docs):
        total = total + lengths[0, r]
        ends.append(total)

    def starts_of(place):
        first = jnp.zeros(place.shape, jnp.int32)
        for r in range(docs):
            first = first + jnp.where(place >= ends[r], lengths[0, r], 0)
        return first

    place = s * tokens + lax.broadcasted_iota(jnp.int32, (tokens, HEAD_SIZE), 0)
    angle = (place - starts_of(place)).astype(jnp.float32) * freq[...]
    lane = lax.broadcasted_iota(jnp.int32, (tokens, HEAD_SIZE), 1)
    cosine[...] = jnp.cos(angle)
    turn = jnp.sin(angle)
    sine[...] = jnp.where(lane < HEAD_SIZE // 2, -turn, turn)

    row = s * tokens + lax.broadcasted_iota(jnp.int32, (tokens, tokens), 0)
    first = starts_of(row)
    for d in range(blocks):
        other = (s - d) * tokens + lax.broadcasted_iota(jnp.int32, (tokens, tokens), 1)
        bias[:, d * tokens : (d + 1) * tokens] = jnp.where(
            (other >= first) & (other <= row), 0.0, MASKED
        )

    which = lax.broadcasted_iota(jnp.int32, (docs, tokens), 0)
    token = s * tokens + lax.broadcasted_iota(jnp.int32, (docs, tokens), 1)
    inside = jnp.zeros((docs, tokens), jnp.float32)
    for r in range(docs):
        answer = jnp.minimum(wanted[0, r], lengths[0, r])
        taken = (which == r) & (token < ends[r]) & (token >= ends[r] - answer)
        inside = jnp.where(taken, 1.0, inside)
    member[...] = inside.astype(jnp.bfloat16)
    which = lax.broadcasted_iota(jnp.int32, (docs, pool_width), 0)
    counted = jnp.ones((docs, pool_width), jnp.int32)
    for r in range(docs):
        counted = jnp.where(which == r, jnp.minimum(wanted[0, r], lengths[0, r]), counted)
    answers[...] = counted.astype(jnp.float32)

    for d in range(1, blocks):

        @pl.when(s < d)
        def _():
            kv[d] = jnp.zeros(kv.shape[1:], kv.dtype)

    own_x.wait()
    for k in range(1, n):
        hid_arrival(k).wait_recv()

    @pl.loop(0, KEY_VALUE_HEADS)
    def _(h):
        w_copy(h, 0).wait()
        w_copy(h, 1).wait()
        product[...] = jnp.dot(
            x[...].reshape(n * tokens, depth), w[h], preferred_element_type=jnp.float32
        ).reshape(n, tokens, 2 * HEAD_SIZE)
        outbox[h] = product[...].astype(jnp.bfloat16)
        own[h] = product[f]
        for k in range(1, n):
            sum_copy(h, k).start()

    def finish(h):
        rows = own[h]
        for k in range(1, n):
            sum_arrival(h, k).wait_recv()
            rows = rows + inbox[h, lax.rem(f + k, n)].astype(jnp.float32)
        key = rows[:, :HEAD_SIZE]
        turned = key * cosine[...] + pltpu.roll(key, HEAD_SIZE // 2, 1) * sine[...]
        kv[0, h, :, :HEAD_SIZE] = turned.astype(jnp.bfloat16)
        kv[0, h, :, HEAD_SIZE:] = rows[:, HEAD_SIZE:].astype(jnp.bfloat16)

        @pl.when(sends_up(0))
        def _():
            up_copy(h, 0).start()

        @pl.when(shares_even(0))
        def _():
            pair_copy(h, 0, 0).start()

    def relay(h, i):
        @pl.when(s >= 2 * i)
        def _():
            up_copy(h, i - 1).wait_recv()

        if i < hops:

            @pl.when(sends_up(i))
            def _():
                up_copy(h, i).start()

            @pl.when(shares_even(i))
            def _():
                pair_copy(h, 2 * i, i).start()

        @pl.when(shares_odd(i - 1))
        def _():
            pair_copy(h, 2 * i, i - 1).start()

    scale = HEAD_SIZE**-0.5 * math.log2(math.e)

    def attend(h):
        for m in range(hops):

            @pl.when(s >= 2 * m + 1)
            def _():
                pair_copy(h, 0, m).wait_recv()

        q_copy(h).wait()
        key = kv[:, h, :, :HEAD_SIZE].reshape(blocks * tokens, HEAD_SIZE)
        value = kv[:, h, :, HEAD_SIZE:].reshape(blocks * tokens, HEAD_SIZE)
        for a in range(q_width // HEAD_SIZE):
            lanes = slice(a * HEAD_SIZE, (a + 1) * HEAD_SIZE)
            scores = (
                lax.dot_general(
                    q[h, :, lanes],
                    key,
                    (((1,), (1,)), ((), ())),
                    preferred_element_type=jnp.float32,
                )
                * scale
                + bias[...]
            )
            peak = jnp.max(scores, axis=-1, keepdims=True)
            probs = jnp.exp2(scores - peak)
            norm = jnp.sum(probs, axis=-1, keepdims=True)
            result = jnp.dot(
                probs.astype(jnp.bfloat16), value, preferred_element_type=jnp.float32
            )
            o[h, :, lanes] = (result / norm).astype(jnp.bfloat16)
        o_copy(h).start()
        sums = jnp.dot(member[...], o[h], preferred_element_type=jnp.float32)
        for m in range(per_head):
            j = h * per_head + m
            part[j] = sums[:, m * pool_width : (m + 1) * pool_width]

            @pl.when(j != s)
            def _():
                pool_copy(j).start()

            @pl.when(j == s)
            def _():
                parts[s] = sums[:, m * pool_width : (m + 1) * pool_width]

    @pl.loop(0, KEY_VALUE_HEADS + hops + 1)
    def _(step):
        @pl.when(step < KEY_VALUE_HEADS)
        def _():
            finish(step)

        for i in range(1, hops + 1):

            @pl.when((step >= i) & (step < KEY_VALUE_HEADS + i))
            def _():
                relay(step - i, i)

        @pl.when(step >= hops + 1)
        def _():
            attend(step - hops - 1)

    @pl.loop(1, ranks)
    def _(k):
        pool_arrival(lax.rem(s + k, ranks)).wait_recv()

    sums = parts[0]
    for i in range(1, ranks):
        sums = sums + parts[i]
    pooled[0] = sums / answers[...]

    for k in range(1, n):
        hid_copy(k).wait_send()

    @pl.loop(0, KEY_VALUE_HEADS)
    def _(h):
        for k in range(1, n):
            sum_copy(h, k).wait_send()
        for i in range(hops):

            @pl.when(sends_up(i))
            def _():
                up_copy(h, i).wait_send()

        for m in range(hops):

            @pl.when(shares_even(m))
            def _():
                pair_copy(h, 2 * m, m).wait_send()

            @pl.when(shares_odd(m))
            def _():
                pair_copy(h, 2 * m + 2, m).wait_send()

        o_copy(h).wait()

    @pl.loop(1, ranks)
    def _(k):
        pool_copy(lax.rem(s + k, ranks)).wait_send()


def on_device(hidden, queries, key_value_weight, doc_lengths, resp_lengths):
    n = lax.axis_size("fsdp")
    ranks = lax.axis_size("seq")
    tokens = hidden.shape[1]
    width = hidden.shape[2]
    depth, kv_cols = key_value_weight.shape
    docs = doc_lengths.shape[1]
    q_cols = queries.shape[2]
    q_width = q_cols // KEY_VALUE_HEADS
    pool_width = q_cols // ranks
    hops = ranks // 4
    blocks = 2 * hops + 1
    heads = KEY_VALUE_HEADS
    if depth % HEAD_SIZE:
        hidden = hidden.reshape(tokens, n, depth).transpose(1, 0, 2)
    power = np.arange(HEAD_SIZE // 2, dtype=np.float64) * 2.0 / HEAD_SIZE
    freq = np.tile(ROPE_BASE**-power, 2).astype(np.float32)[None]
    any_space = pl.BlockSpec(memory_space=pl.ANY)
    smem = pl.BlockSpec(memory_space=pltpu.SMEM)
    vmem = pl.BlockSpec(memory_space=pltpu.VMEM)
    dma = pltpu.SemaphoreType.DMA
    bf16, f32 = jnp.bfloat16, jnp.float32
    return pl.pallas_call(
        functools.partial(kernel, n, ranks, hops),
        out_shape=(
            jax.ShapeDtypeStruct((1, tokens, q_cols), bf16),
            jax.ShapeDtypeStruct((1, docs, pool_width), f32),
        ),
        in_specs=[any_space, any_space, any_space, smem, smem, vmem],
        out_specs=(any_space, vmem),
        scratch_shapes=[
            pltpu.VMEM((n, tokens, depth), bf16),
            pltpu.VMEM((heads, depth, 2 * HEAD_SIZE), bf16),
            pltpu.VMEM((heads, tokens, q_width), bf16),
            pltpu.VMEM((n, tokens, 2 * HEAD_SIZE), f32),
            pltpu.VMEM((heads, tokens, 2 * HEAD_SIZE), f32),
            pltpu.VMEM((heads, n, tokens, 2 * HEAD_SIZE), bf16),
            pltpu.VMEM((heads, n, tokens, 2 * HEAD_SIZE), bf16),
            pltpu.VMEM((blocks, heads, tokens, 2 * HEAD_SIZE), bf16),
            pltpu.VMEM((heads, tokens, q_width), bf16),
            pltpu.VMEM((tokens, blocks * tokens), f32),
            pltpu.VMEM((tokens, HEAD_SIZE), f32),
            pltpu.VMEM((tokens, HEAD_SIZE), f32),
            pltpu.VMEM((docs, tokens), bf16),
            pltpu.VMEM((docs, pool_width), f32),
            pltpu.VMEM((ranks, docs, pool_width), f32),
            pltpu.VMEM((ranks, docs, pool_width), f32),
            dma,
            dma((heads, 2)),
            dma((heads,)),
            dma((heads,)),
            dma((n,)),
            dma((n,)),
            dma((heads, n)),
            dma((heads, n)),
            dma((heads, hops)),
            dma((heads, hops)),
            dma((heads, hops)),
            dma((heads, hops)),
            dma((ranks,)),
            dma((ranks,)),
        ],
        compiler_params=pltpu.CompilerParams(
            collective_id=0, has_side_effects=True, vmem_limit_bytes=56 * 2**20
        ),
    )(hidden, queries, key_value_weight, doc_lengths, resp_lengths, jnp.asarray(freq))


def solution(mesh):
    in_specs = (
        P("fsdp", "seq", None),
        P("fsdp", "seq", None),
        P("fsdp", None),
        P("fsdp", None),
        P("fsdp", None),
    )
    out_specs = (P("fsdp", "seq", None), P("fsdp", None, "seq"))
    return jax.shard_map(
        on_device, mesh=mesh, in_specs=in_specs, out_specs=out_specs, check_vma=False
    )
```

```python
import functools
import math

import jax
import jax.numpy as jnp
import numpy as np
from jax import lax
from jax.experimental import pallas as pl
from jax.experimental.pallas import tpu as pltpu
from jax.sharding import PartitionSpec as P

HEAD_SIZE = 128
KEY_VALUE_HEADS = 8
ROPE_BASE = 1000000.0
MASKED = -1e30
MESH = pl.DeviceIdType.MESH


def kernel(
    n,
    ranks,
    hops,
    hidden,
    queries,
    weight,
    lengths,
    wanted,
    freq,
    attended,
    pooled,
    raw,
    x,
    w,
    q,
    product,
    own,
    outbox,
    inbox,
    middle,
    outbox2,
    inbox2,
    kv,
    o,
    bias,
    cosine,
    sine,
    member,
    answers,
    part,
    parts,
    x_sem,
    w_sem,
    q_sem,
    o_sem,
    hid_send,
    hid_recv,
    sum_send,
    sum_recv,
    sum2_send,
    sum2_recv,
    up_send,
    up_recv,
    pair_send,
    pair_recv,
    pool_send,
    pool_recv,
):
    f = lax.axis_index("fsdp")
    s = lax.axis_index("seq")
    odd = lax.rem(s, 2)
    partner = s + 1 - 2 * odd
    above = lax.rem(s + 2, ranks)
    side = math.isqrt(n)
    fx = lax.rem(f, side)
    fy = lax.div(f, side)
    tokens = x.shape[1]
    depth = x.shape[2]
    half = weight.shape[1] // 2
    q_width = q.shape[1] // KEY_VALUE_HEADS
    docs = lengths.shape[1]
    blocks = kv.shape[0]
    pool_width = part.shape[2]
    per_head = q_width // pool_width

    def columns(start, size):
        return pl.ds(pl.multiple_of(start, HEAD_SIZE), size)

    def features(j):
        if len(raw.shape) == 3:
            return raw.at[j]
        return raw.at[:, columns(j * depth, depth)]

    pieces = x_sem.shape[0]

    def chunk(source, target, sems, i):
        rows = source.shape[0] // pieces
        part_rows = pl.ds(i * rows, rows)
        return pltpu.make_async_copy(source.at[part_rows], target.at[part_rows], sems.at[i])

    def x_copy(i):
        if len(raw.shape) == 3:
            rows = tokens // pieces
            part_rows = pl.ds(i * rows, rows)
            return pltpu.make_async_copy(
                hidden.at[:, part_rows], raw.at[:, part_rows], x_sem.at[i]
            )
        return chunk(hidden.at[0], raw, x_sem, i)

    def w_copy(i):
        return chunk(weight, w, w_sem, i)

    def q_copy(i):
        return chunk(queries.at[0], q, q_sem, i)

    def o_copy(h):
        return pltpu.make_async_copy(
            o.at[h], attended.at[0, :, columns(h * q_width, q_width)], o_sem.at[h]
        )

    def hid_copy(k):
        j = lax.rem(f + k, n)
        return pltpu.make_async_remote_copy(
            src_ref=features(j),
            dst_ref=x.at[f],
            send_sem=hid_send.at[k],
            recv_sem=hid_recv.at[f],
            device_id=(j, s),
            device_id_type=MESH,
        )

    def hid_arrival(k):
        i = lax.rem(f + k, n)
        return pltpu.make_async_remote_copy(
            src_ref=x.at[i],
            dst_ref=x.at[i],
            send_sem=hid_send.at[k],
            recv_sem=hid_recv.at[i],
            device_id=(i, s),
            device_id_type=MESH,
        )

    def place_of(h):
        p = lax.rem(h, 2)
        return p * fy + (1 - p) * fx, p * fx + (1 - p) * fy

    def index_of(h, u, v):
        p = lax.rem(h, 2)
        return p * (u * side + v) + (1 - p) * (v * side + u)

    def sum_copy(h, k):
        u, v = place_of(h)
        to = lax.rem(u + k, side)
        return pltpu.make_async_remote_copy(
            src_ref=outbox.at[h, to],
            dst_ref=inbox.at[h, u],
            send_sem=sum_send.at[h, k],
            recv_sem=sum_recv.at[h, u],
            device_id=(index_of(h, to, v), s),
            device_id_type=MESH,
        )

    def sum_arrival(h, k):
        u, v = place_of(h)
        come = lax.rem(u + k, side)
        return pltpu.make_async_remote_copy(
            src_ref=outbox.at[h, come],
            dst_ref=inbox.at[h, come],
            send_sem=sum_send.at[h, k],
            recv_sem=sum_recv.at[h, come],
            device_id=(index_of(h, come, v), s),
            device_id_type=MESH,
        )

    def sum2_copy(h, k):
        u, v = place_of(h)
        to = lax.rem(v + k, side)
        return pltpu.make_async_remote_copy(
            src_ref=outbox2.at[h, k],
            dst_ref=inbox2.at[h, v],
            send_sem=sum2_send.at[h, k],
            recv_sem=sum2_recv.at[h, v],
            device_id=(index_of(h, u, to), s),
            device_id_type=MESH,
        )

    def sum2_arrival(h, k):
        u, v = place_of(h)
        come = lax.rem(v + k, side)
        return pltpu.make_async_remote_copy(
            src_ref=outbox2.at[h, k],
            dst_ref=inbox2.at[h, come],
            send_sem=sum2_send.at[h, k],
            recv_sem=sum2_recv.at[h, come],
            device_id=(index_of(h, u, come), s),
            device_id_type=MESH,
        )

    def up_copy(h, i):
        return pltpu.make_async_remote_copy(
            src_ref=kv.at[2 * i, h],
            dst_ref=kv.at[2 * i + 2, h],
            send_sem=up_send.at[h, i],
            recv_sem=up_recv.at[h, i],
            device_id=(f, above),
            device_id_type=MESH,
        )

    def pair_copy(h, source, m):
        return pltpu.make_async_remote_copy(
            src_ref=kv.at[source, h],
            dst_ref=kv.at[2 * m + 1, h],
            send_sem=pair_send.at[h, m],
            recv_sem=pair_recv.at[h, m],
            device_id=(f, partner),
            device_id_type=MESH,
        )

    def pool_copy(j):
        return pltpu.make_async_remote_copy(
            src_ref=part.at[j],
            dst_ref=parts.at[s],
            send_sem=pool_send.at[j],
            recv_sem=pool_recv.at[s],
            device_id=(f, j),
            device_id_type=MESH,
        )

    def pool_arrival(i):
        return pltpu.make_async_remote_copy(
            src_ref=part.at[i],
            dst_ref=parts.at[i],
            send_sem=pool_send.at[i],
            recv_sem=pool_recv.at[i],
            device_id=(f, i),
            device_id_type=MESH,
        )

    def sends_up(i):
        return (s + 2 < ranks) & (s >= 2 * i)

    def shares_even(m):
        return (odd == 0) & (s >= 2 * m)

    def shares_odd(m):
        return (odd == 1) & (s >= 2 * m + 2)

    for i in range(pieces):
        x_copy(i).start()
    for i in range(pieces):
        w_copy(i).start()
    for i in range(pieces):
        q_copy(i).start()

    barrier = pltpu.get_barrier_semaphore()
    for k in range(1, n):
        pl.semaphore_signal(
            barrier, inc=1, device_id=(lax.rem(f + k, n), s), device_id_type=MESH
        )
    for k in range(1, ranks):
        pl.semaphore_signal(
            barrier, inc=1, device_id=(f, lax.rem(s + k, ranks)), device_id_type=MESH
        )
    for i in range(pieces):
        x_copy(i).wait()
    pl.semaphore_wait(barrier, n + ranks - 2)
    for k in range(1, n):
        hid_copy(k).start()

    ends = []
    total = jnp.int32(0)
    for r in range(docs):
        total = total + lengths[0, r]
        ends.append(total)

    def starts_of(place):
        first = jnp.zeros(place.shape, jnp.int32)
        for r in range(docs):
            first = first + jnp.where(place >= ends[r], lengths[0, r], 0)
        return first

    place = s * tokens + lax.broadcasted_iota(jnp.int32, (tokens, HEAD_SIZE), 0)
    angle = (place - starts_of(place)).astype(jnp.float32) * freq[...]
    lane = lax.broadcasted_iota(jnp.int32, (tokens, HEAD_SIZE), 1)
    cosine[...] = jnp.cos(angle)
    turn = jnp.sin(angle)
    sine[...] = jnp.where(lane < HEAD_SIZE // 2, -turn, turn)

    row = s * tokens + lax.broadcasted_iota(jnp.int32, (tokens, tokens), 0)
    first = starts_of(row)
    for d in range(blocks):
        other = (s - d) * tokens + lax.broadcasted_iota(jnp.int32, (tokens, tokens), 1)
        bias[:, d * tokens : (d + 1) * tokens] = jnp.where(
            (other >= first) & (other <= row), 0.0, MASKED
        )

    which = lax.broadcasted_iota(jnp.int32, (docs, tokens), 0)
    token = s * tokens + lax.broadcasted_iota(jnp.int32, (docs, tokens), 1)
    inside = jnp.zeros((docs, tokens), jnp.float32)
    for r in range(docs):
        answer = jnp.minimum(wanted[0, r], lengths[0, r])
        taken = (which == r) & (token < ends[r]) & (token >= ends[r] - answer)
        inside = jnp.where(taken, 1.0, inside)
    member[...] = inside.astype(jnp.bfloat16)
    which = lax.broadcasted_iota(jnp.int32, (docs, pool_width), 0)
    counted = jnp.ones((docs, pool_width), jnp.int32)
    for r in range(docs):
        counted = jnp.where(which == r, jnp.minimum(wanted[0, r], lengths[0, r]), counted)
    answers[...] = counted.astype(jnp.float32)

    for d in range(1, blocks):

        @pl.when(s < d)
        def _():
            kv[d] = jnp.zeros(kv.shape[1:], kv.dtype)

    x[f] = features(f)[...]
    for i in range(pieces):
        w_copy(i).wait()
    for i in range(pieces):
        q_copy(i).wait()
    for k in range(1, n):
        hid_arrival(k).wait_recv()

    def project(h):
        strips = [
            w[:, columns(side_of * half + h * HEAD_SIZE, HEAD_SIZE)] for side_of in range(2)
        ]
        product[...] = jnp.dot(
            x[...].reshape(n * tokens, depth),
            jnp.concatenate(strips, axis=1),
            preferred_element_type=jnp.float32,
        ).reshape(n, tokens, 2 * HEAD_SIZE)
        u, v = place_of(h)
        for k in range(1, side):
            to = lax.rem(u + k, side)
            for l in range(side):
                outbox[h, to, l] = product[index_of(h, to, l)].astype(jnp.bfloat16)
            sum_copy(h, k).start()
        for k in range(side):
            own[h, k] = product[index_of(h, u, lax.rem(v + k, side))]

    def combine(h):
        u, v = place_of(h)
        for k in range(1, side):
            sum_arrival(h, k).wait_recv()
        for m in list(range(1, side)) + [0]:
            rows = own[h, m]
            for k in range(1, side):
                rows = rows + inbox[h, lax.rem(u + k, side), lax.rem(v + m, side)].astype(
                    jnp.float32
                )
            if m:
                outbox2[h, m] = rows.astype(jnp.bfloat16)
                sum2_copy(h, m).start()
            else:
                middle[h] = rows

    def finish(h):
        u, v = place_of(h)
        rows = middle[h]
        for k in range(1, side):
            sum2_arrival(h, k).wait_recv()
            rows = rows + inbox2[h, lax.rem(v + k, side)].astype(jnp.float32)
        key = rows[:, :HEAD_SIZE]
        turned = key * cosine[...] + pltpu.roll(key, HEAD_SIZE // 2, 1) * sine[...]
        kv[0, h, :, :HEAD_SIZE] = turned.astype(jnp.bfloat16)
        kv[0, h, :, HEAD_SIZE:] = rows[:, HEAD_SIZE:].astype(jnp.bfloat16)

        @pl.when(sends_up(0))
        def _():
            up_copy(h, 0).start()

        @pl.when(shares_even(0))
        def _():
            pair_copy(h, 0, 0).start()

    def relay(h, i):
        @pl.when(s >= 2 * i)
        def _():
            up_copy(h, i - 1).wait_recv()

        if i < hops:

            @pl.when(sends_up(i))
            def _():
                up_copy(h, i).start()

            @pl.when(shares_even(i))
            def _():
                pair_copy(h, 2 * i, i).start()

        @pl.when(shares_odd(i - 1))
        def _():
            pair_copy(h, 2 * i, i - 1).start()

    scale = HEAD_SIZE**-0.5 * math.log2(math.e)

    def attend(h):
        for m in range(hops):

            @pl.when(s >= 2 * m + 1)
            def _():
                pair_copy(h, 0, m).wait_recv()

        key = kv[:, h, :, :HEAD_SIZE].reshape(blocks * tokens, HEAD_SIZE)
        value = kv[:, h, :, HEAD_SIZE:].reshape(blocks * tokens, HEAD_SIZE)
        shared = q_width // HEAD_SIZE
        query = jnp.concatenate(
            [q[:, columns(h * q_width + a * HEAD_SIZE, HEAD_SIZE)] for a in range(shared)],
            axis=0,
        )
        scores = lax.dot_general(
            query, key, (((1,), (1,)), ((), ())), preferred_element_type=jnp.float32
        ).reshape(shared, tokens, blocks * tokens)
        scores = scores * scale + bias[...][None]
        peak = jnp.max(scores, axis=-1, keepdims=True)
        probs = jnp.exp2(scores - peak)
        norm = jnp.sum(probs, axis=-1, keepdims=True)
        result = jnp.dot(
            probs.astype(jnp.bfloat16).reshape(shared * tokens, blocks * tokens),
            value,
            preferred_element_type=jnp.float32,
        ).reshape(shared, tokens, HEAD_SIZE)
        result = (result / norm).astype(jnp.bfloat16)
        for a in range(shared):
            o[h, :, a * HEAD_SIZE : (a + 1) * HEAD_SIZE] = result[a]
        o_copy(h).start()
        sums = jnp.dot(member[...], o[h], preferred_element_type=jnp.float32)
        for m in range(per_head):
            j = h * per_head + m
            part[j] = sums[:, m * pool_width : (m + 1) * pool_width]

            @pl.when(j != s)
            def _():
                pool_copy(j).start()

            @pl.when(j == s)
            def _():
                parts[s] = sums[:, m * pool_width : (m + 1) * pool_width]

    stages = [(0, project), (2, combine), (3, finish)]
    stages += [(3 + i, functools.partial(relay, i=i)) for i in range(1, hops + 1)]
    stages += [(4 + hops, attend)]

    @pl.loop(0, KEY_VALUE_HEADS + 4 + hops)
    def _(step):
        for lag, stage in stages:

            @pl.when((step >= lag) & (step < KEY_VALUE_HEADS + lag))
            def _():
                stage(step - lag)

    @pl.loop(1, ranks)
    def _(k):
        pool_arrival(lax.rem(s + k, ranks)).wait_recv()

    sums = parts[0]
    for i in range(1, ranks):
        sums = sums + parts[i]
    pooled[0] = sums / answers[...]

    for k in range(1, n):
        hid_copy(k).wait_send()

    @pl.loop(0, KEY_VALUE_HEADS)
    def _(h):
        for k in range(1, side):
            sum_copy(h, k).wait_send()
            sum2_copy(h, k).wait_send()
        for i in range(hops):

            @pl.when(sends_up(i))
            def _():
                up_copy(h, i).wait_send()

        for m in range(hops):

            @pl.when(shares_even(m))
            def _():
                pair_copy(h, 2 * m, m).wait_send()

            @pl.when(shares_odd(m))
            def _():
                pair_copy(h, 2 * m + 2, m).wait_send()

        o_copy(h).wait()

    @pl.loop(1, ranks)
    def _(k):
        pool_copy(lax.rem(s + k, ranks)).wait_send()


def on_device(hidden, queries, key_value_weight, doc_lengths, resp_lengths):
    n = lax.axis_size("fsdp")
    ranks = lax.axis_size("seq")
    tokens = hidden.shape[1]
    width = hidden.shape[2]
    depth, kv_cols = key_value_weight.shape
    docs = doc_lengths.shape[1]
    q_cols = queries.shape[2]
    q_width = q_cols // KEY_VALUE_HEADS
    pool_width = q_cols // ranks
    hops = ranks // 4
    blocks = 2 * hops + 1
    heads = KEY_VALUE_HEADS
    if depth % HEAD_SIZE:
        hidden = hidden.reshape(tokens, n, depth).transpose(1, 0, 2)
    power = np.arange(HEAD_SIZE // 2, dtype=np.float64) * 2.0 / HEAD_SIZE
    freq = np.tile(ROPE_BASE**-power, 2).astype(np.float32)[None]
    side = math.isqrt(n)
    assert side * side == n
    pieces = 4
    any_space = pl.BlockSpec(memory_space=pl.ANY)
    smem = pl.BlockSpec(memory_space=pltpu.SMEM)
    vmem = pl.BlockSpec(memory_space=pltpu.VMEM)
    dma = pltpu.SemaphoreType.DMA
    bf16, f32 = jnp.bfloat16, jnp.float32
    return pl.pallas_call(
        functools.partial(kernel, n, ranks, hops),
        out_shape=(
            jax.ShapeDtypeStruct((1, tokens, q_cols), bf16),
            jax.ShapeDtypeStruct((1, docs, pool_width), f32),
        ),
        in_specs=[any_space, any_space, any_space, smem, smem, vmem],
        out_specs=(any_space, vmem),
        scratch_shapes=[
            pltpu.VMEM(hidden.shape[-3 if depth % HEAD_SIZE else -2 :], bf16),
            pltpu.VMEM((n, tokens, depth), bf16),
            pltpu.VMEM((depth, kv_cols), bf16),
            pltpu.VMEM((tokens, q_cols), bf16),
            pltpu.VMEM((n, tokens, 2 * HEAD_SIZE), f32),
            pltpu.VMEM((heads, side, tokens, 2 * HEAD_SIZE), f32),
            pltpu.VMEM((heads, side, side, tokens, 2 * HEAD_SIZE), bf16),
            pltpu.VMEM((heads, side, side, tokens, 2 * HEAD_SIZE), bf16),
            pltpu.VMEM((heads, tokens, 2 * HEAD_SIZE), f32),
            pltpu.VMEM((heads, side, tokens, 2 * HEAD_SIZE), bf16),
            pltpu.VMEM((heads, side, tokens, 2 * HEAD_SIZE), bf16),
            pltpu.VMEM((blocks, heads, tokens, 2 * HEAD_SIZE), bf16),
            pltpu.VMEM((heads, tokens, q_width), bf16),
            pltpu.VMEM((tokens, blocks * tokens), f32),
            pltpu.VMEM((tokens, HEAD_SIZE), f32),
            pltpu.VMEM((tokens, HEAD_SIZE), f32),
            pltpu.VMEM((docs, tokens), bf16),
            pltpu.VMEM((docs, pool_width), f32),
            pltpu.VMEM((ranks, docs, pool_width), f32),
            pltpu.VMEM((ranks, docs, pool_width), f32),
            dma((pieces,)),
            dma((pieces,)),
            dma((pieces,)),
            dma((heads,)),
            dma((n,)),
            dma((n,)),
            dma((heads, side)),
            dma((heads, side)),
            dma((heads, side)),
            dma((heads, side)),
            dma((heads, hops)),
            dma((heads, hops)),
            dma((heads, hops)),
            dma((heads, hops)),
            dma((ranks,)),
            dma((ranks,)),
        ],
        compiler_params=pltpu.CompilerParams(
            collective_id=0, has_side_effects=True, vmem_limit_bytes=56 * 2**20
        ),
    )(hidden, queries, key_value_weight, doc_lengths, resp_lengths, jnp.asarray(freq))


def solution(mesh):
    in_specs = (
        P("fsdp", "seq", None),
        P("fsdp", "seq", None),
        P("fsdp", None),
        P("fsdp", None),
        P("fsdp", None),
    )
    out_specs = (P("fsdp", "seq", None), P("fsdp", None, "seq"))
    return jax.shard_map(
        on_device, mesh=mesh, in_specs=in_specs, out_specs=out_specs, check_vma=False
    )
```

```python
import functools
import math

import jax
import jax.numpy as jnp
import numpy as np
from jax import lax
from jax.experimental import pallas as pl
from jax.experimental.pallas import tpu as pltpu
from jax.sharding import PartitionSpec as P

HEAD_SIZE = 128
KEY_VALUE_HEADS = 8
ROPE_BASE = 1000000.0
MASKED = -1e30
MESH = pl.DeviceIdType.MESH


def kernel(
    n,
    ranks,
    hops,
    hidden,
    queries,
    weight,
    lengths,
    wanted,
    freq,
    attended,
    pooled,
    x,
    w,
    q,
    product,
    own,
    outbox,
    inbox,
    middle,
    outbox2,
    inbox2,
    kv,
    o,
    bias,
    cosine,
    sine,
    member,
    answers,
    part,
    parts,
    x_sem,
    w_sem,
    q_sem,
    o_sem,
    hid_send,
    hid_recv,
    sum_send,
    sum_recv,
    sum2_send,
    sum2_recv,
    up_send,
    up_recv,
    pair_send,
    pair_recv,
    pool_send,
    pool_recv,
):
    f = lax.axis_index("fsdp")
    s = lax.axis_index("seq")
    odd = lax.rem(s, 2)
    partner = s + 1 - 2 * odd
    above = lax.rem(s + 2, ranks)
    side = math.isqrt(n)
    fx = lax.rem(f, side)
    fy = lax.div(f, side)
    halves = x.shape[0]
    span = x.shape[2]
    tokens = halves * span
    depth = x.shape[3]
    units = halves * KEY_VALUE_HEADS
    half = weight.shape[1] // 2
    q_width = q.shape[1] // KEY_VALUE_HEADS
    docs = lengths.shape[1]
    blocks = kv.shape[0]
    pool_width = part.shape[2]
    per_head = q_width // pool_width

    def columns(start, size):
        return pl.ds(pl.multiple_of(start, HEAD_SIZE), size)

    def half_head(e):
        return lax.div(e, KEY_VALUE_HEADS), lax.rem(e, KEY_VALUE_HEADS)

    def features(c, j):
        rows = pl.ds(pl.multiple_of(c * span, span), span)
        if depth % HEAD_SIZE:
            return hidden.at[j, rows]
        return hidden.at[0, rows, columns(j * depth, depth)]

    pieces = w_sem.shape[0]

    def x_copy(c):
        return pltpu.make_async_copy(features(c, f), x.at[c, f], x_sem.at[c])

    def chunk(source, target, sems, i):
        rows = source.shape[0] // pieces
        part_rows = pl.ds(i * rows, rows)
        return pltpu.make_async_copy(source.at[part_rows], target.at[part_rows], sems.at[i])

    def w_copy(i):
        return chunk(weight, w, w_sem, i)

    def q_copy(i):
        return chunk(queries.at[0], q, q_sem, i)

    def o_copy(h):
        return pltpu.make_async_copy(
            o.at[h], attended.at[0, :, columns(h * q_width, q_width)], o_sem.at[h]
        )

    def hid_copy(c, k):
        j = lax.rem(f + k, n)
        return pltpu.make_async_remote_copy(
            src_ref=features(c, j),
            dst_ref=x.at[c, f],
            send_sem=hid_send.at[c, k],
            recv_sem=hid_recv.at[c, f],
            device_id=(j, s),
            device_id_type=MESH,
        )

    def hid_arrival(c, k):
        i = lax.rem(f + k, n)
        return pltpu.make_async_remote_copy(
            src_ref=x.at[c, i],
            dst_ref=x.at[c, i],
            send_sem=hid_send.at[c, k],
            recv_sem=hid_recv.at[c, i],
            device_id=(i, s),
            device_id_type=MESH,
        )

    def place_of(h):
        p = lax.rem(h, 2)
        return p * fy + (1 - p) * fx, p * fx + (1 - p) * fy

    def index_of(h, u, v):
        p = lax.rem(h, 2)
        return p * (u * side + v) + (1 - p) * (v * side + u)

    def sum_copy(h, k):
        u, v = place_of(h)
        to = lax.rem(u + k, side)
        return pltpu.make_async_remote_copy(
            src_ref=outbox.at[h, to],
            dst_ref=inbox.at[h, u],
            send_sem=sum_send.at[h, k],
            recv_sem=sum_recv.at[h, u],
            device_id=(index_of(h, to, v), s),
            device_id_type=MESH,
        )

    def sum_arrival(h, k):
        u, v = place_of(h)
        come = lax.rem(u + k, side)
        return pltpu.make_async_remote_copy(
            src_ref=outbox.at[h, come],
            dst_ref=inbox.at[h, come],
            send_sem=sum_send.at[h, k],
            recv_sem=sum_recv.at[h, come],
            device_id=(index_of(h, come, v), s),
            device_id_type=MESH,
        )

    def sum2_copy(h, k):
        u, v = place_of(h)
        to = lax.rem(v + k, side)
        return pltpu.make_async_remote_copy(
            src_ref=outbox2.at[h, k],
            dst_ref=inbox2.at[h, v],
            send_sem=sum2_send.at[h, k],
            recv_sem=sum2_recv.at[h, v],
            device_id=(index_of(h, u, to), s),
            device_id_type=MESH,
        )

    def sum2_arrival(h, k):
        u, v = place_of(h)
        come = lax.rem(v + k, side)
        return pltpu.make_async_remote_copy(
            src_ref=outbox2.at[h, k],
            dst_ref=inbox2.at[h, come],
            send_sem=sum2_send.at[h, k],
            recv_sem=sum2_recv.at[h, come],
            device_id=(index_of(h, u, come), s),
            device_id_type=MESH,
        )

    def up_copy(e, i):
        c, h = half_head(e)
        return pltpu.make_async_remote_copy(
            src_ref=kv.at[2 * i, h, c],
            dst_ref=kv.at[2 * i + 2, h, c],
            send_sem=up_send.at[e, i],
            recv_sem=up_recv.at[e, i],
            device_id=(f, above),
            device_id_type=MESH,
        )

    def pair_copy(e, source, m):
        c, h = half_head(e)
        return pltpu.make_async_remote_copy(
            src_ref=kv.at[source, h, c],
            dst_ref=kv.at[2 * m + 1, h, c],
            send_sem=pair_send.at[e, m],
            recv_sem=pair_recv.at[e, m],
            device_id=(f, partner),
            device_id_type=MESH,
        )

    def pool_copy(j):
        return pltpu.make_async_remote_copy(
            src_ref=part.at[j],
            dst_ref=parts.at[s],
            send_sem=pool_send.at[j],
            recv_sem=pool_recv.at[s],
            device_id=(f, j),
            device_id_type=MESH,
        )

    def pool_arrival(i):
        return pltpu.make_async_remote_copy(
            src_ref=part.at[i],
            dst_ref=parts.at[i],
            send_sem=pool_send.at[i],
            recv_sem=pool_recv.at[i],
            device_id=(f, i),
            device_id_type=MESH,
        )

    def sends_up(i):
        return (s + 2 < ranks) & (s >= 2 * i)

    def shares_even(m):
        return (odd == 0) & (s >= 2 * m)

    def shares_odd(m):
        return (odd == 1) & (s >= 2 * m + 2)


    barrier = pltpu.get_barrier_semaphore()
    for k in range(1, n):
        pl.semaphore_signal(
            barrier, inc=1, device_id=(lax.rem(f + k, n), s), device_id_type=MESH
        )
    for k in range(1, ranks):
        pl.semaphore_signal(
            barrier, inc=1, device_id=(f, lax.rem(s + k, ranks)), device_id_type=MESH
        )
    pl.semaphore_wait(barrier, n + ranks - 2)
    for k in range(1, n):
        hid_copy(0, k).start()
    for c in range(halves):
        x_copy(c).start()
    for i in range(pieces):
        w_copy(i).start()
    for i in range(pieces):
        q_copy(i).start()

    ends = []
    total = jnp.int32(0)
    for r in range(docs):
        total = total + lengths[0, r]
        ends.append(total)

    def starts_of(place):
        first = jnp.zeros(place.shape, jnp.int32)
        for r in range(docs):
            first = first + jnp.where(place >= ends[r], lengths[0, r], 0)
        return first

    place = s * tokens + lax.broadcasted_iota(jnp.int32, (tokens, HEAD_SIZE), 0)
    angle = (place - starts_of(place)).astype(jnp.float32) * freq[...]
    lane = lax.broadcasted_iota(jnp.int32, (tokens, HEAD_SIZE), 1)
    cosine[...] = jnp.cos(angle).reshape(cosine.shape)
    turn = jnp.sin(angle)
    sine[...] = jnp.where(lane < HEAD_SIZE // 2, -turn, turn).reshape(sine.shape)

    row = s * tokens + lax.broadcasted_iota(jnp.int32, (tokens, tokens), 0)
    first = starts_of(row)
    for d in range(blocks):
        other = (s - d) * tokens + lax.broadcasted_iota(jnp.int32, (tokens, tokens), 1)
        bias[:, d * tokens : (d + 1) * tokens] = jnp.where(
            (other >= first) & (other <= row), 0.0, MASKED
        )

    which = lax.broadcasted_iota(jnp.int32, (docs, tokens), 0)
    token = s * tokens + lax.broadcasted_iota(jnp.int32, (docs, tokens), 1)
    inside = jnp.zeros((docs, tokens), jnp.float32)
    for r in range(docs):
        answer = jnp.minimum(wanted[0, r], lengths[0, r])
        taken = (which == r) & (token < ends[r]) & (token >= ends[r] - answer)
        inside = jnp.where(taken, 1.0, inside)
    member[...] = inside.astype(jnp.bfloat16)
    which = lax.broadcasted_iota(jnp.int32, (docs, pool_width), 0)
    counted = jnp.ones((docs, pool_width), jnp.int32)
    for r in range(docs):
        counted = jnp.where(which == r, jnp.minimum(wanted[0, r], lengths[0, r]), counted)
    answers[...] = counted.astype(jnp.float32)

    for d in range(1, blocks):

        @pl.when(s < d)
        def _():
            kv[d] = jnp.zeros(kv.shape[1:], kv.dtype)

    for c in range(halves):
        x_copy(c).wait()
    for i in range(pieces):
        w_copy(i).wait()
    for i in range(pieces):
        q_copy(i).wait()
    def project(e):
        c, h = half_head(e)

        @pl.when(h == 0)
        def _():
            for k in range(1, n):
                hid_arrival(c, k).wait_recv()

            @pl.when(c + 1 < halves)
            def _():
                for k in range(1, n):
                    hid_copy(c + 1, k).start()

        strips = [
            w[:, columns(side_of * half + h * HEAD_SIZE, HEAD_SIZE)] for side_of in range(2)
        ]
        product[...] = jnp.dot(
            x[c].reshape(n * span, depth),
            jnp.concatenate(strips, axis=1),
            preferred_element_type=jnp.float32,
        ).reshape(n, span, 2 * HEAD_SIZE)
        u, v = place_of(e)
        for k in range(1, side):
            to = lax.rem(u + k, side)
            for l in range(side):
                outbox[e, to, l] = product[index_of(e, to, l)].astype(jnp.bfloat16)
            sum_copy(e, k).start()
        for k in range(side):
            own[e, k] = product[index_of(e, u, lax.rem(v + k, side))]

    def combine(e):
        u, v = place_of(e)
        for k in range(1, side):
            sum_arrival(e, k).wait_recv()
        for m in list(range(1, side)) + [0]:
            rows = own[e, m]
            for k in range(1, side):
                rows = rows + inbox[e, lax.rem(u + k, side), lax.rem(v + m, side)].astype(
                    jnp.float32
                )
            if m:
                outbox2[e, m] = rows.astype(jnp.bfloat16)
                sum2_copy(e, m).start()
            else:
                middle[e] = rows

    def finish(e):
        c, h = half_head(e)
        u, v = place_of(e)
        rows = middle[e]
        for k in range(1, side):
            sum2_arrival(e, k).wait_recv()
            rows = rows + inbox2[e, lax.rem(v + k, side)].astype(jnp.float32)
        key = rows[:, :HEAD_SIZE]
        turned = key * cosine[c] + pltpu.roll(key, HEAD_SIZE // 2, 1) * sine[c]
        kv[0, h, c, :, :HEAD_SIZE] = turned.astype(jnp.bfloat16)
        kv[0, h, c, :, HEAD_SIZE:] = rows[:, HEAD_SIZE:].astype(jnp.bfloat16)

        @pl.when(sends_up(0))
        def _():
            up_copy(e, 0).start()

        @pl.when(shares_even(0))
        def _():
            pair_copy(e, 0, 0).start()

    def relay(e, i):
        @pl.when(s >= 2 * i)
        def _():
            up_copy(e, i - 1).wait_recv()

        if i < hops:

            @pl.when(sends_up(i))
            def _():
                up_copy(e, i).start()

            @pl.when(shares_even(i))
            def _():
                pair_copy(e, 2 * i, i).start()

        @pl.when(shares_odd(i - 1))
        def _():
            pair_copy(e, 2 * i, i - 1).start()

    scale = HEAD_SIZE**-0.5 * math.log2(math.e)

    def attend(e):
        h = lax.rem(e, KEY_VALUE_HEADS)
        for m in range(hops):

            @pl.when(s >= 2 * m + 1)
            def _():
                for c in range(halves):
                    pair_copy(c * KEY_VALUE_HEADS + h, 0, m).wait_recv()

        key = kv[:, h, :, :, :HEAD_SIZE].reshape(blocks * tokens, HEAD_SIZE)
        value = kv[:, h, :, :, HEAD_SIZE:].reshape(blocks * tokens, HEAD_SIZE)
        shared = q_width // HEAD_SIZE
        query = jnp.concatenate(
            [q[:, columns(h * q_width + a * HEAD_SIZE, HEAD_SIZE)] for a in range(shared)],
            axis=0,
        )
        scores = lax.dot_general(
            query, key, (((1,), (1,)), ((), ())), preferred_element_type=jnp.float32
        ).reshape(shared, tokens, blocks * tokens)
        scores = scores * scale + bias[...][None]
        peak = jnp.max(scores, axis=-1, keepdims=True)
        probs = jnp.exp2(scores - peak)
        norm = jnp.sum(probs, axis=-1, keepdims=True)
        result = jnp.dot(
            probs.astype(jnp.bfloat16).reshape(shared * tokens, blocks * tokens),
            value,
            preferred_element_type=jnp.float32,
        ).reshape(shared, tokens, HEAD_SIZE)
        result = (result / norm).astype(jnp.bfloat16)
        for a in range(shared):
            o[h, :, a * HEAD_SIZE : (a + 1) * HEAD_SIZE] = result[a]
        o_copy(h).start()
        sums = jnp.dot(member[...], o[h], preferred_element_type=jnp.float32)
        for m in range(per_head):
            j = h * per_head + m
            part[j] = sums[:, m * pool_width : (m + 1) * pool_width]

            @pl.when(j != s)
            def _():
                pool_copy(j).start()

            @pl.when(j == s)
            def _():
                parts[s] = sums[:, m * pool_width : (m + 1) * pool_width]

    stages = [(0, 0, project), (2, 0, combine), (3, 0, finish)]
    stages += [(3 + i, 0, functools.partial(relay, i=i)) for i in range(1, hops + 1)]
    stages += [(4 + hops, units - KEY_VALUE_HEADS, attend)]

    @pl.loop(0, units + 4 + hops)
    def _(step):
        for lag, least, stage in stages:

            @pl.when((step >= lag + least) & (step < units + lag))
            def _():
                stage(step - lag)

    for c in range(halves):
        for k in range(1, n):
            hid_copy(c, k).wait_send()

    @pl.loop(0, units)
    def _(e):
        for k in range(1, side):
            sum_copy(e, k).wait_send()
            sum2_copy(e, k).wait_send()
        for i in range(hops):

            @pl.when(sends_up(i))
            def _():
                up_copy(e, i).wait_send()

        for m in range(hops):

            @pl.when(shares_even(m))
            def _():
                pair_copy(e, 2 * m, m).wait_send()

            @pl.when(shares_odd(m))
            def _():
                pair_copy(e, 2 * m + 2, m).wait_send()

    @pl.loop(1, ranks)
    def _(k):
        pool_arrival(lax.rem(s + k, ranks)).wait_recv()

    sums = parts[0]
    for i in range(1, ranks):
        sums = sums + parts[i]
    pooled[0] = sums / answers[...]

    @pl.loop(0, KEY_VALUE_HEADS)
    def _(h):
        o_copy(h).wait()

    @pl.loop(1, ranks)
    def _(k):
        pool_copy(lax.rem(s + k, ranks)).wait_send()


def hand_over(attended, pooled, attended_out, pooled_out, held, held_pooled, sems):
    pieces = sems.shape[0] - 1
    rows = attended.shape[1] // pieces
    chunks = [pl.ds(i * rows, rows) for i in range(pieces)]
    here = [attended.at[:, c] for c in chunks] + [pooled]
    kept = [held.at[:, c] for c in chunks] + [held_pooled]
    there = [attended_out.at[:, c] for c in chunks] + [pooled_out]
    arrive = [
        pltpu.make_async_copy(here[i], kept[i], sems.at[i, 0]) for i in range(pieces + 1)
    ]
    leave = [
        pltpu.make_async_copy(kept[i], there[i], sems.at[i, 1]) for i in range(pieces + 1)
    ]
    for i in range(pieces + 1):
        arrive[i].start()
    for i in range(pieces + 1):
        arrive[i].wait()
        leave[i].start()
    for i in range(pieces + 1):
        leave[i].wait()


def on_device(hidden, queries, key_value_weight, doc_lengths, resp_lengths):
    n = lax.axis_size("fsdp")
    ranks = lax.axis_size("seq")
    tokens = hidden.shape[1]
    width = hidden.shape[2]
    depth, kv_cols = key_value_weight.shape
    docs = doc_lengths.shape[1]
    q_cols = queries.shape[2]
    q_width = q_cols // KEY_VALUE_HEADS
    pool_width = q_cols // ranks
    hops = ranks // 4
    blocks = 2 * hops + 1
    heads = KEY_VALUE_HEADS
    if depth % HEAD_SIZE:
        hidden = hidden.reshape(tokens, n, depth).transpose(1, 0, 2)
    power = np.arange(HEAD_SIZE // 2, dtype=np.float64) * 2.0 / HEAD_SIZE
    freq = np.tile(ROPE_BASE**-power, 2).astype(np.float32)[None]
    side = math.isqrt(n)
    assert side * side == n
    pieces = 4
    halves = 1
    span = tokens // halves
    units = halves * heads
    pair = 2 * HEAD_SIZE
    any_space = pl.BlockSpec(memory_space=pl.ANY)
    smem = pl.BlockSpec(memory_space=pltpu.SMEM)
    vmem = pl.BlockSpec(memory_space=pltpu.VMEM)
    dma = pltpu.SemaphoreType.DMA
    bf16, f32 = jnp.bfloat16, jnp.float32
    results = pl.pallas_call(
        functools.partial(kernel, n, ranks, hops),
        out_shape=(
            jax.ShapeDtypeStruct((1, tokens, q_cols), bf16),
            jax.ShapeDtypeStruct((1, docs, pool_width), f32),
        ),
        in_specs=[any_space, any_space, any_space, smem, smem, vmem],
        out_specs=(any_space, vmem),
        scratch_shapes=[
            pltpu.VMEM((halves, n, span, depth), bf16),
            pltpu.VMEM((depth, kv_cols), bf16),
            pltpu.VMEM((tokens, q_cols), bf16),
            pltpu.VMEM((n, span, pair), f32),
            pltpu.VMEM((units, side, span, pair), f32),
            pltpu.VMEM((units, side, side, span, pair), bf16),
            pltpu.VMEM((units, side, side, span, pair), bf16),
            pltpu.VMEM((units, span, pair), f32),
            pltpu.VMEM((units, side, span, pair), bf16),
            pltpu.VMEM((units, side, span, pair), bf16),
            pltpu.VMEM((blocks, heads, halves, span, pair), bf16),
            pltpu.VMEM((heads, tokens, q_width), bf16),
            pltpu.VMEM((tokens, blocks * tokens), f32),
            pltpu.VMEM((halves, span, HEAD_SIZE), f32),
            pltpu.VMEM((halves, span, HEAD_SIZE), f32),
            pltpu.VMEM((docs, tokens), bf16),
            pltpu.VMEM((docs, pool_width), f32),
            pltpu.VMEM((ranks, docs, pool_width), f32),
            pltpu.VMEM((ranks, docs, pool_width), f32),
            dma((halves,)),
            dma((pieces,)),
            dma((pieces,)),
            dma((heads,)),
            dma((halves, n)),
            dma((halves, n)),
            dma((units, side)),
            dma((units, side)),
            dma((units, side)),
            dma((units, side)),
            dma((units, hops)),
            dma((units, hops)),
            dma((units, hops)),
            dma((units, hops)),
            dma((ranks,)),
            dma((ranks,)),
        ],
        compiler_params=pltpu.CompilerParams(
            collective_id=0, has_side_effects=True, vmem_limit_bytes=56 * 2**20
        ),
    )(hidden, queries, key_value_weight, doc_lengths, resp_lengths, jnp.asarray(freq))
    return pl.pallas_call(
        hand_over,
        out_shape=tuple(jax.ShapeDtypeStruct(r.shape, r.dtype) for r in results),
        in_specs=[any_space, any_space],
        out_specs=(any_space, any_space),
        scratch_shapes=[pltpu.VMEM(r.shape, r.dtype) for r in results] + [dma((pieces + 1, 2))],
    )(*results)


def solution(mesh):
    in_specs = (
        P("fsdp", "seq", None),
        P("fsdp", "seq", None),
        P("fsdp", None),
        P("fsdp", None),
        P("fsdp", None),
    )
    out_specs = (P("fsdp", "seq", None), P("fsdp", None, "seq"))
    return jax.shard_map(
        on_device, mesh=mesh, in_specs=in_specs, out_specs=out_specs, check_vma=False
    )
```
